32 devices in a mesh: fsdp: 8 (over z, core), batch: 4 (over y, x).
Axes of the slice: x: 2, y: 2, z: 4, core: 2. Of those that a mesh axis runs over, the one named last changes fastest.
Arguments:
- latents: bfloat16 [4, 8, 1024, 640], P('batch', 'fsdp'), may hold values from -6 to 6
- norm_gain: float32 [640], replicated, may hold values from 0.25 to 1.75
- second_gain: float32 [640], replicated, may hold values from 0.25 to 1.75
- spatial_w: bfloat16 [9, 640, 640], P(None, None, 'fsdp'), may hold values from -0.078125 to 0.078125
- temporal_w: bfloat16 [3, 640, 640], P(None, None, 'fsdp'), may hold values from -0.125 to 0.125
- critic_w: bfloat16 [4, 640, 640], P('batch'), may hold values from -0.25 to 0.25
- critic_head: float32 [4, 640], P('batch'), may hold values from -6 to 6
- targets: int32 [4, 32, 1], P('batch'), may hold values from 0 to 3; in each aligned block of 32 rows (0 to 31, 32 to 63, ..., all dimensions but the last counted through in order) at most 16 rows name the same one
- feasible: int32 [4, 8], P('batch', 'fsdp'), may hold values 0 or 1
Outputs:
- guided: bfloat16 [4, 8, 1024, 640], P('batch', 'fsdp')
The draws below stay inside these ranges and needn't reach their ends.
Inputs may be any that keep to these rules, and one draw needn't show every extreme that they name: `targets`: among one candidate's 32 rows no critic group is named more than 16 times.
All inputs are finite; a program needn't handle non-finite values. No bound on the sum of `feasible` on one device may be relied on, other than what follows from the above.
Results may differ from the reference program's by a relative error of at most 0.0065.
Values may be sent and summed in bfloat16 or wider, within the bound.
A program may use at most 128 MiB of HBM per device.

```python
import math
import jax
import jax.numpy as jnp
import numpy as np
from jax import lax

C = 640
HID = 640
GROUPS = 32
IMG_ROWS = 32
IMG_COLS = 32
PIX = 1024
FRAMES = 8
CANDIDATES = 4
CAP = 16
N_BATCH = 4


def touch_ends(entries, stream_key, least, largest):
    longest = entries.shape.index(max(entries.shape))
    spots = []
    for shift in (0, 1):
        where = [jax.random.randint(jax.random.fold_in(stream_key, axis), (), 0, length) for axis, length in enumerate(entries.shape)]
        where[longest] = (where[longest] + shift) % entries.shape[longest]
        spots.append(tuple(where))
    return entries.at[spots[0]].set(least).at[spots[1]].set(largest)


def block_levels(key, shape, split, smallest, top_value):
    level, own = 1.0, jax.random.fold_in(key, 6)
    for position, blocks in split:
        steps = jnp.exp(jax.random.uniform(jax.random.fold_in(own, position), (blocks,), jnp.float32, smallest / len(split), top_value / len(split)))
        level = level * jnp.repeat(steps, shape[position] // blocks).reshape([-1 if axis == position else 1 for axis in range(len(shape))])
    return level


def assign_block(rng, own, number, rows, count, top, reach, skew):
    order = jax.random.permutation(rng, count)
    heavy_load, common = load_shares(count, rows * top, reach, skew, True), load_shares(count, rows * top, reach, skew, False)
    places = jnp.arange(count)

    def named(lengths, rotation):
        used = int((lengths > 0).sum())
        fixed = max(1, used // 4)
        shifted = fixed + (places - fixed + rotation * (used - fixed)) % max(1, count - fixed)
        return jnp.zeros((count,), jnp.int32).at[order[jnp.where(places < fixed, places, shifted)]].set(jnp.asarray(lengths, jnp.int32))

    lengths = jnp.where(number % 4 == 0, named(heavy_load, number // 4), named(common, number - number // 4 - 1))
    mixed = jax.random.permutation(jax.random.fold_in(own, 3), count)
    giver, sink = mixed[0:count // 2 * 2:2], mixed[1:count // 2 * 2:2]
    room = jnp.minimum(lengths[giver] - 1, reach - lengths[sink]) // 2
    room = jnp.where((giver == order[0]) | (sink == order[0]) | (lengths[sink] == 0), 0, jnp.maximum(room, 0))
    shifted = jax.random.randint(jax.random.fold_in(own, 4), (count // 2,), 0, 1 << 20) % (room + 1)
    lengths = lengths.at[giver].add(-shifted).at[sink].add(shifted)
    members = jnp.searchsorted(jnp.cumsum(lengths), jnp.arange(rows * top), side="right").astype(jnp.int32)
    listing = members.reshape(top, rows).T
    listing = listing[jax.random.permutation(jax.random.fold_in(own, 1), rows)]
    rotation = jax.random.randint(jax.random.fold_in(own, 2), (rows, 1), 0, top)
    return jnp.take_along_axis(listing, (jnp.arange(top)[None, :] + rotation) % top, axis=1)


def load_shares(number_of, total, bound, skew, full):
    loads = [(1 << 20) // math.isqrt(grade ** skew) + 1 for grade in range(1, number_of + 1)]
    largest = bound if full else min(bound, max(-(-total // number_of), total * loads[0] // sum(loads)))
    least = 1 if total - largest >= number_of - 1 else 0
    given, rest = [largest] + [least] * (number_of - 1), total - largest - least * (number_of - 1)
    while rest > 0:
        free = [i for i in range(1, number_of) if given[i] < largest] or [i for i in range(1, number_of) if given[i] < bound]
        whole, budget = sum([loads[i] for i in free]), rest
        for i in free:
            extra = min(bound - given[i], max(1, budget * loads[i] // whole), rest)
            given[i] = given[i] + extra
            rest = rest - extra
    return np.array(given)


def scatter_about(rng, shape, scale, bound, pieces=(), dtype=jnp.bfloat16):
    array = scale * jax.random.normal(rng, shape, jnp.float32)
    if pieces:
        array = array * block_levels(rng, shape, pieces, -0.22, 0.18)
    return jnp.clip(array, -bound, bound).astype(dtype)


def setup_inputs(seed: int = 0) -> dict:
    key_of = jax.random.split(jax.random.key(seed), 10)
    latents = scatter_about(key_of[0], (CANDIDATES, FRAMES, PIX, C), 1.0, 6.0, ((0, 4), (1, 8)))
    norm_gain = jnp.clip(1.0 + 0.15 * jax.random.normal(key_of[1], (C,), jnp.float32), 0.25, 1.75)
    second_gain = jnp.clip(1.0 + 0.15 * jax.random.normal(key_of[2], (C,), jnp.float32), 0.25, 1.75)
    spatial_w = scatter_about(key_of[3], (9, C, C), (9 * C) ** -0.5, 0.078125, ((2, 8),))
    temporal_w = scatter_about(key_of[4], (3, C, C), (3 * C) ** -0.5, 0.125, ((2, 8),))
    critic_w = scatter_about(key_of[5], (N_BATCH, C, HID), C ** -0.5, 0.25, ((0, 4),))
    critic_head = scatter_about(key_of[6], (N_BATCH, HID), 1.0, 6.0, ((0, 4),), jnp.float32)
    targets_keys = jax.random.split(jax.random.fold_in(key_of[7], 1), CANDIDATES * IMG_ROWS // IMG_ROWS)
    targets_turns = jax.random.permutation(jax.random.fold_in(key_of[7], 3), CANDIDATES * IMG_ROWS // IMG_ROWS)
    targets = jax.vmap(lambda own, number: assign_block(jax.random.fold_in(key_of[7], 2), own, number, IMG_ROWS, N_BATCH, 1, CAP, 1))(targets_keys, targets_turns).reshape((CANDIDATES, IMG_ROWS, 1))
    feasible = touch_ends((jax.random.randint(key_of[8], (CANDIDATES, FRAMES), 0, 4) < 3).astype(jnp.int32), jax.random.fold_in(key_of[8], 1), 0, 1)
    return dict(latents=latents, norm_gain=norm_gain, second_gain=second_gain, spatial_w=spatial_w, temporal_w=temporal_w, critic_w=critic_w, critic_head=critic_head, targets=targets, feasible=feasible)


def group_silu(values, gain):
    shape = values.shape
    width = shape[-1]
    grouped = values.astype(jnp.float32).reshape(shape[0], shape[1], GROUPS, width // GROUPS)
    center = lax.optimization_barrier(jnp.mean(grouped, axis=(1, 3), keepdims=True))
    spread = lax.optimization_barrier(jnp.mean((grouped - center) ** 2, axis=(1, 3), keepdims=True))
    normed = ((grouped - center) * lax.rsqrt(spread + 1e-05)).reshape(shape) * gain
    return jax.nn.silu(normed).astype(jnp.bfloat16)

def one_plan(latent, target_rows, listed, norm_gain, second_gain, spatial_w, temporal_w, critic_w, critic_head):
    frames_all = latent.shape[0]
    width = latent.shape[-1]
    first = group_silu(latent, norm_gain)
    padded = jnp.pad(first.reshape(frames_all, IMG_ROWS, IMG_COLS, width), ((0, 0), (1, 1), (1, 1), (0, 0)))
    mixed = jnp.zeros((frames_all * PIX, width), jnp.float32)
    for offset in range(9):
        row_off, col_off = divmod(offset, 3)
        window = padded[:, row_off:row_off + IMG_ROWS, col_off:col_off + IMG_COLS].reshape(-1, width)
        mixed = mixed + jnp.dot(window, spatial_w[offset], preferred_element_type=jnp.float32)
    section = (latent.astype(jnp.float32) + mixed.reshape(latent.shape)).astype(jnp.bfloat16)
    second = group_silu(section, second_gain)
    framed = jnp.pad(second, ((1, 1), (0, 0), (0, 0)))
    motion = jnp.zeros((frames_all * PIX, width), jnp.float32)
    for tap in range(3):
        motion = motion + jnp.dot(framed[tap:tap + frames_all].reshape(-1, width), temporal_w[tap], preferred_element_type=jnp.float32)
    denoised = (section.astype(jnp.float32) + motion.reshape(latent.shape)).astype(jnp.bfloat16)
    chosen = target_rows[:, 0]
    picked = critic_w[chosen].astype(jnp.float32)
    heads = critic_head[chosen]
    rowwise = denoised.reshape(frames_all, IMG_ROWS, IMG_COLS, width).astype(jnp.float32)
    pre = jnp.einsum('frpc,rch->frph', rowwise, picked)
    slope = ((1.0 - jnp.tanh(pre) ** 2) * heads[None, :, None, :]).astype(jnp.bfloat16)
    grad = jnp.einsum('frph,rch->frpc', slope.astype(jnp.float32), picked).astype(jnp.bfloat16)
    scale = listed.astype(jnp.float32)[:, None, None]
    return (denoised.astype(jnp.float32) - scale * grad.astype(jnp.float32).reshape(latent.shape)).astype(jnp.bfloat16)

def reference(latents, norm_gain, second_gain, spatial_w, temporal_w, critic_w, critic_head, targets, feasible):

    def step_one(items):
        latent, target_rows, listed = items
        return one_plan(latent, target_rows, listed, norm_gain, second_gain, spatial_w, temporal_w, critic_w, critic_head)
    return lax.map(step_one, (latents, targets, feasible))
```

```python
import functools

import jax
import jax.numpy as jnp
from jax import lax
from jax.experimental import pallas as pl
from jax.experimental.pallas import tpu as pltpu
from jax.sharding import PartitionSpec as P

GROUPS = 32
IMG_ROWS = 32
IMG_COLS = 32
PIX = 1024
F32 = jnp.float32
BF16 = jnp.bfloat16
MESH = pl.DeviceIdType.MESH
NT = (((1,), (1,)), ((), ()))


def ring_gather(piece, axis, dim):
    size, me = lax.axis_size(axis), lax.axis_index(axis)
    length = piece.shape[dim]
    shape = piece.shape[:dim] + (length * size,) + piece.shape[dim + 1 :]
    whole = jnp.zeros(shape, piece.dtype)
    whole = lax.dynamic_update_slice_in_dim(whole, piece, me * length, dim)
    for step in range(1, size):
        piece = lax.ppermute(piece, axis, [(i, (i + 1) % size) for i in range(size)])
        owner = lax.rem(me - step + size, size)
        whole = lax.dynamic_update_slice_in_dim(whole, piece, owner * length, dim)
    return whole


def with_halo(array, sides, width):
    for axis, dim in sides:
        size, length = (lax.axis_size(axis), array.shape[dim])
        up = [(i, (i + 1) % size) for i in range(size - 1)]
        down = [(j, i) for i, j in up]
        last = lax.slice_in_dim(array, length - width, length, axis=dim)
        leading = lax.slice_in_dim(array, 0, width, axis=dim)
        before = lax.ppermute(last, axis, up)
        after = lax.ppermute(leading, axis, down)
        array = jnp.concatenate([before, array, after], axis=dim)
    return array


def group_silu(values, gain):
    shape = values.shape
    width = shape[-1]
    grouped = values.astype(jnp.float32).reshape(-1, shape[-2], GROUPS, width // GROUPS)
    center = jnp.mean(grouped, axis=(1, 3), keepdims=True)
    spread = jnp.mean((grouped - center) ** 2, axis=(1, 3), keepdims=True)
    normed = ((grouped - center) * lax.rsqrt(spread + 1e-05)).reshape(shape) * gain
    return jax.nn.silu(normed).astype(jnp.bfloat16)


def per_device(
    latents, norm_gain, second_gain, spatial_w, temporal_w, critic_w, critic_head, targets, feasible
):
    cands = latents.shape[0]
    width = latents.shape[-1]
    first = group_silu(latents, norm_gain)
    padded = jnp.pad(
        first.reshape(cands, IMG_ROWS, IMG_COLS, width), ((0, 0), (1, 1), (1, 1), (0, 0))
    )
    piece = ring_gather(spatial_w, "fsdp", 2)
    total = jnp.zeros((cands * PIX, piece.shape[2]), jnp.float32)
    for offset in range(9):
        row_off, col_off = divmod(offset, 3)
        window = padded[:, row_off : row_off + IMG_ROWS, col_off : col_off + IMG_COLS].reshape(
            -1, width
        )
        total = total + jnp.dot(window, piece[offset], preferred_element_type=jnp.float32)
    mixed = total
    section = (latents.astype(jnp.float32) + mixed.reshape(latents.shape)).astype(jnp.bfloat16)
    second = group_silu(section, second_gain)
    beside_all = with_halo(second, (("fsdp", 1),), 1)
    piece = ring_gather(temporal_w, "fsdp", 2)
    total = jnp.zeros((cands * PIX, piece.shape[2]), jnp.float32)
    for tap in range(3):
        total = total + jnp.dot(
            beside_all[:, tap].reshape(-1, width), piece[tap], preferred_element_type=jnp.float32
        )
    denoised = (section.astype(jnp.float32) + total.reshape(latents.shape)).astype(jnp.bfloat16)
    groups = lax.axis_size("batch")
    capacity = max(2, 2 * IMG_ROWS // groups)
    slots = cands * capacity
    flat_targets = targets.reshape(-1)
    chosen = (flat_targets[:, None] == jnp.arange(groups, dtype=jnp.int32)[None, :]).astype(
        jnp.int32
    )
    spot = jnp.arange(chosen.shape[0], dtype=jnp.int32)
    before = (spot[None, :, None] < spot[:, None, None]).astype(jnp.int32)
    earlier = jnp.sum(before * chosen[None], axis=1)
    slot_of = jnp.sum(earlier * chosen, axis=1)
    live = jnp.repeat(feasible.reshape(-1), IMG_ROWS) > 0
    position = flat_targets * slots + slot_of
    placing = (
        (jnp.arange(groups * slots, dtype=jnp.int32)[:, None] == position[None, :]) & live[None, :]
    ).astype(jnp.bfloat16)
    rows = denoised.reshape(cands * IMG_ROWS, IMG_COLS * width)
    outgoing = (
        jnp.dot(placing, rows, preferred_element_type=jnp.float32)
        .astype(jnp.bfloat16)
        .reshape(groups, slots, IMG_COLS * width)
    )
    weights = ring_gather(critic_w, "batch", 0)
    heads = ring_gather(critic_head, "batch", 0)
    count = weights.shape[0]
    block = outgoing.reshape(count, -1, width)
    pre = jnp.einsum("gtc,gch->gth", block, weights, preferred_element_type=jnp.float32)
    slope = ((1.0 - jnp.tanh(pre) ** 2) * heads[:, None, :]).astype(jnp.bfloat16)
    grads = jnp.einsum("gth,gch->gtc", slope, weights, preferred_element_type=jnp.float32).astype(
        jnp.bfloat16
    )
    returned = grads.reshape(count, slots, -1)
    back = jnp.dot(
        placing.T, returned.reshape(groups * slots, -1), preferred_element_type=jnp.float32
    )
    guided = (rows.astype(jnp.float32) - back).astype(jnp.bfloat16)
    return guided.reshape(latents.shape)


def moments(sums, spread_matrix):
    wide = jnp.broadcast_to(sums, (8, sums.shape[1]))
    return jnp.dot(
        wide, spread_matrix, precision=lax.Precision.HIGHEST, preferred_element_type=F32
    )[0:1]


def fused_kernel(
    latents, gain1, gain2, mine, critic_mine, heads_mine, same, targets, feasible,
    out,
    weights, critics, heads, shifted, mixed, section, frames, denoised,
    up_send, down_send, z_recv, a_send, a_recv, b_send, b_recv, s_send, s_recv,
    ca_send, ca_recv, cb_send, cb_recv, cs_send, cs_recv, h_send, h_recv,
    f_send, f_recv, local_sem,
):
    C = latents.shape[1]
    part = mine.shape[1]
    fs, b = lax.axis_index("fsdp"), lax.axis_index("batch")
    z, c = fs // 2, fs % 2
    zs = 4
    x_peer, y_peer = b + 1 - 2 * (b % 2), b + 2 - 4 * (b // 2)
    peer_a = (1 - c) * x_peer + c * y_peer
    peer_b = c * x_peer + (1 - c) * y_peer
    peer_d = 3 - b
    sib = (fs + 1 - 2 * c, b)
    up, down = (fs + 2, b), (fs - 2, b)
    to_a, to_b, to_d = (fs, peer_a), (fs, peer_b), (fs, peer_d)
    far = (fs + 2 * c - 1, b)
    has_up, has_down = z < zs - 1, z > 0
    has_far = ((c == 1) & (z < zs - 1)) | ((c == 0) & (z > 0))

    barrier = pltpu.get_barrier_semaphore()
    for to in (sib, to_a, to_b, to_d):
        pl.semaphore_signal(barrier, inc=1, device_id=to, device_id_type=MESH)

    @pl.when(has_up)
    def _():
        pl.semaphore_signal(barrier, inc=1, device_id=up, device_id_type=MESH)

    @pl.when(has_down)
    def _():
        pl.semaphore_signal(barrier, inc=1, device_id=down, device_id_type=MESH)

    @pl.when(has_far)
    def _():
        pl.semaphore_signal(barrier, inc=1, device_id=far, device_id_type=MESH)

    met = 4 + has_up.astype(jnp.int32) + has_down.astype(jnp.int32) + has_far.astype(jnp.int32)
    pl.semaphore_wait(barrier, met)

    def send(src, dst, ss, rs, to):
        return pltpu.make_async_remote_copy(
            src_ref=src, dst_ref=dst, send_sem=ss, recv_sem=rs, device_id=to, device_id_type=MESH
        )

    def slab(quarter, level, core, t):
        rows = pl.ds(pl.multiple_of((2 * level + core) * part, 16), part)
        return weights.at[quarter, rows, pl.ds(t * C, C)]

    def shard(level, core, t):
        rows = pl.ds(pl.multiple_of((2 * level + core) * part, 16), part)
        return weights.at[:, rows, pl.ds(t * C, C)]

    def own(quarter, t):
        return mine.at[quarter, :, pl.ds(t * C, C)]

    def z_copy(level, t, to, sems, first):
        src = own(b, t) if first else slab(b, level, c, t)
        return send(src, slab(b, level, c, t), sems.at[level, t], z_recv.at[level, t], to)

    def a_copy(level, t):
        return send(slab(b, level, c, t), slab(b, level, c, t), a_send.at[level, t], a_recv.at[level, t], to_a)

    def b_copy(level, t, j):
        q = b if j == 0 else peer_a
        return send(slab(q, level, c, t), slab(q, level, c, t), b_send.at[level, t, j], b_recv.at[level, t, j], to_b)

    def s_copy(level, t, first=False):
        src = mine.at[:, :, pl.ds(t * C, C)] if first else shard(level, c, t)
        return send(src, shard(level, c, t), s_send.at[level, t], s_recv.at[level, t], sib)

    for t in range(3):

        @pl.when(has_up)
        def _():
            z_copy(z, t, up, up_send, True).start()

        @pl.when(has_down)
        def _():
            z_copy(z, t, down, down_send, True).start()

        s_copy(z, t, True).start()
    into = pltpu.make_async_copy(
        mine, weights.at[:, pl.ds(pl.multiple_of(fs * part, 16), part), :], local_sem.at[0]
    )
    into.start()
    own_critic = pltpu.make_async_copy(critic_mine, critics.at[b], local_sem.at[1])
    own_critic.start()
    own_head = pltpu.make_async_copy(heads_mine, heads.at[b], local_sem.at[2])
    own_head.start()

    def h_copy(j, to):
        return send(heads_mine, heads.at[b], h_send.at[j], h_recv.at[j], to)

    for j, to in enumerate((to_a, to_b, to_d)):
        h_copy(j, to).start()

    scale = 1.0 / (PIX * (C // GROUPS))

    def stats(load):
        def add(r, total):
            v = load(r)
            return total + jnp.sum(v, axis=0, keepdims=True)

        center = moments(lax.fori_loop(0, IMG_ROWS, add, jnp.zeros((1, C), F32)), same[...]) * scale

        def add_sq(r, total):
            v = load(r) - center
            return total + jnp.sum(v * v, axis=0, keepdims=True)

        var = moments(lax.fori_loop(0, IMG_ROWS, add_sq, jnp.zeros((1, C), F32)), same[...]) * scale
        return center, lax.rsqrt(var + 1e-05)

    def at_row(r):
        return pl.ds(pl.multiple_of(r * IMG_COLS, IMG_COLS), IMG_COLS)

    def load_latent(r):
        return latents[at_row(r), :].astype(F32)

    center1, inv1 = stats(load_latent)
    edge = jnp.zeros((IMG_COLS, 3 * C), BF16)
    shifted[0:IMG_COLS, :] = edge
    shifted[PIX + IMG_COLS : PIX + 2 * IMG_COLS, :] = edge
    column = lax.broadcasted_iota(jnp.int32, (IMG_COLS, C), 0)

    @pl.loop(0, IMG_ROWS)
    def _(r):
        v = (load_latent(r) - center1) * inv1 * gain1[...]
        v = v / (1.0 + jnp.exp(-v))
        where = pl.ds(pl.multiple_of((r + 1) * IMG_COLS, IMG_COLS), IMG_COLS)
        shifted[where, 0:C] = jnp.where(column == 0, 0.0, pltpu.roll(v, 1, 0)).astype(BF16)
        shifted[where, C : 2 * C] = v.astype(BF16)
        shifted[where, 2 * C : 3 * C] = jnp.where(
            column == IMG_COLS - 1, 0.0, pltpu.roll(v, IMG_COLS - 1, 0)
        ).astype(BF16)

    MB = 256
    width = 2 * part

    def conv(level):
        rows = pl.ds(pl.multiple_of(level * width, 16), width)

        @pl.loop(0, PIX // MB)
        def _(m):
            total = jnp.zeros((MB, width), F32)
            for a in range(3):
                x = shifted[pl.ds(pl.multiple_of(m * MB + a * IMG_COLS, IMG_COLS), MB), :]
                total = total + lax.dot_general(x, weights[a, rows, :], NT, preferred_element_type=F32)
            mixed[level, pl.ds(pl.multiple_of(m * MB, MB), MB), :] = total

    k0 = jnp.where(z < 2, z + 1, z - 1)
    k1 = jnp.where(z == 0, 2, jnp.where(z == 1, 0, jnp.where(z == 2, 3, 1)))
    k2 = jnp.where(z < 2, 3, 0)
    steps = [(k, t) for k in (k0, k1, k2) for t in range(3)]
    half = C // 2

    def crit(who):
        return critics.at[who, pl.ds(pl.multiple_of(c * half, 16), half), :]

    def ca_copy():
        return send(critic_mine.at[pl.ds(pl.multiple_of(c * half, 16), half), :], crit(b), ca_send, ca_recv, to_a)

    def cb_copy(j):
        if j == 0:
            src, who = critic_mine.at[pl.ds(pl.multiple_of(c * half, 16), half), :], b
        else:
            src, who = crit(peer_a), peer_a
        return send(src, crit(who), cb_send.at[j], cb_recv.at[j], to_b)

    def cs_copy(j):
        who = (peer_a, peer_b, peer_d)[j]
        return send(crit(who), crit(who), cs_send.at[j], cs_recv.at[j], sib)

    into.wait()
    for i in range(len(steps) + 2):
        if i < len(steps):
            k, t = steps[i]
            z_copy(k, t, up, up_send, False).wait_recv()

            @pl.when((k < z) & has_up)
            def _():
                z_copy(k, t, up, up_send, False).start()

            @pl.when((k > z) & has_down)
            def _():
                z_copy(k, t, down, down_send, False).start()

            a_copy(k, t).start()
        if 1 <= i <= len(steps):
            k, t = steps[i - 1]
            a_copy(k, t).wait_recv()
            for j in range(2):
                b_copy(k, t, j).start()
        if i >= 2:
            k, t = steps[i - 2]
            for j in range(2):
                b_copy(k, t, j).wait_recv()
            s_copy(k, t).start()
        if i == 2:
            for t in range(3):
                s_copy(z, t).wait_recv()
            conv(z)
        if i == 6:
            for t in range(3):
                s_copy(k0, t).wait_recv()
            conv(k0)
        if i == 9:
            ca_copy().start()
            cb_copy(0).start()
            for t in range(3):
                s_copy(k1, t).wait_recv()
            conv(k1)
    for t in range(3):
        s_copy(k2, t).wait_recv()
    ca_copy().wait_recv()
    cb_copy(1).start()
    conv(k2)

    @pl.loop(0, IMG_ROWS)
    def _(r):
        here = at_row(r)
        whole = jnp.concatenate([mixed[l, here, :] for l in range(zs)], axis=1)
        section[here, :] = (load_latent(r) + whole).astype(BF16)

    def load_section(r):
        return section[at_row(r), :].astype(F32)

    center2, inv2 = stats(load_section)
    parts = 4
    block = PIX // parts

    def f_copy(j, p, to):
        slot = c if j == 0 else 1 - c
        rows = pl.ds(p * block, block)
        return send(frames.at[1, rows, :], frames.at[slot * 2, rows, :], f_send.at[j, p], f_recv.at[j, p], to)

    @pl.when(jnp.logical_not(has_far))
    def _():
        @pl.loop(0, IMG_ROWS)
        def _(r):
            frames[2 * c, at_row(r), :] = jnp.zeros((IMG_COLS, C), BF16)

    for p in range(parts):

        @pl.loop(p * (IMG_ROWS // parts), (p + 1) * (IMG_ROWS // parts))
        def _(r):
            v = (load_section(r) - center2) * inv2 * gain2[...]
            frames[1, at_row(r), :] = (v / (1.0 + jnp.exp(-v))).astype(BF16)

        @pl.when(has_far)
        def _():
            f_copy(1, p, far).start()

        f_copy(0, p, sib).start()

    for j in range(2):
        cb_copy(j).wait_recv()
    for j in range(3):
        cs_copy(j).start()

    own_critic.wait()
    own_head.wait()
    for j, to in enumerate((to_a, to_b, to_d)):
        h_copy(j, to).wait_recv()
    for j in range(3):
        cs_copy(j).wait_recv()
    listed = feasible[0].astype(F32)
    for p in range(parts):
        f_copy(0, p, sib).wait_recv()

        @pl.when(has_far)
        def _():
            f_copy(1, p, far).wait_recv()

        rows = slice(p * block, (p + 1) * block)
        total = lax.dot_general(frames[0, rows, :], weights[3, :, 0:C], NT, preferred_element_type=F32)
        for j in (1, 2):
            total = total + lax.dot_general(
                frames[j, rows, :], weights[3, :, j * C : (j + 1) * C], NT, preferred_element_type=F32
            )
        denoised[rows, :] = (section[rows, :].astype(F32) + total).astype(BF16)

        @pl.loop(p * (IMG_ROWS // parts), (p + 1) * (IMG_ROWS // parts))
        def _(r):
            here = at_row(r)
            g = targets[r]
            w = critics[g]
            hd = heads[g]
            d = denoised[here, :]
            pre = jnp.tanh(jnp.dot(d, w, preferred_element_type=F32))
            slope = ((1.0 - pre * pre) * hd[0:1, :]).astype(BF16)
            grad = lax.dot_general(slope, w, NT, preferred_element_type=F32).astype(BF16)
            out[here, :] = (d.astype(F32) - listed * grad.astype(F32)).astype(BF16)

    for t in range(3):
        for level in (z, k0, k1, k2):
            first = level is z

            @pl.when(has_up & (level <= z))
            def _():
                z_copy(level, t, up, up_send, first).wait_send()

            @pl.when(has_down & (level >= z))
            def _():
                z_copy(level, t, down, down_send, first).wait_send()

            s_copy(level, t, first).wait_send()
            if not first:
                a_copy(level, t).wait_send()
                for j in range(2):
                    b_copy(level, t, j).wait_send()
    ca_copy().wait_send()
    for j in range(2):
        cb_copy(j).wait_send()
    for j, to in enumerate((to_a, to_b, to_d)):
        h_copy(j, to).wait_send()
        cs_copy(j).wait_send()
    for p in range(parts):
        f_copy(0, p, sib).wait_send()

        @pl.when(has_far)
        def _():
            f_copy(1, p, far).wait_send()


def fused(
    latents, norm_gain, second_gain, spatial_w, temporal_w, critic_w, critic_head, targets, feasible
):
    C = latents.shape[-1]
    part = spatial_w.shape[-1]
    mine = jnp.concatenate([spatial_w, temporal_w]).reshape(4, 3, C, part)
    mine = mine.transpose(0, 3, 1, 2).reshape(4, part, 3 * C)
    group = jnp.arange(C, dtype=jnp.int32) // (C // GROUPS)
    same = (group[:, None] == group[None, :]).astype(F32)
    vmem = pl.BlockSpec(memory_space=pltpu.VMEM)
    smem = pl.BlockSpec(memory_space=pltpu.SMEM)
    dma = pltpu.SemaphoreType.DMA
    guided = pl.pallas_call(
        fused_kernel,
        out_shape=jax.ShapeDtypeStruct((PIX, C), BF16),
        in_specs=[vmem] * 7 + [smem] * 2,
        out_specs=vmem,
        scratch_shapes=[
            pltpu.VMEM((4, C, 3 * C), BF16),
            pltpu.VMEM((4, C, C), BF16),
            pltpu.VMEM((4, 8, C), F32),
            pltpu.VMEM((PIX + 2 * IMG_COLS, 3 * C), BF16),
            pltpu.VMEM((4, PIX, 2 * part), F32),
            pltpu.VMEM((PIX, C), BF16),
            pltpu.VMEM((3, PIX, C), BF16),
            pltpu.VMEM((PIX, C), BF16),
            dma((4, 3)), dma((4, 3)), dma((4, 3)),
            dma((4, 3)), dma((4, 3)),
            dma((4, 3, 2)), dma((4, 3, 2)),
            dma((4, 3)), dma((4, 3)),
            dma, dma, dma((2,)), dma((2,)), dma((3,)), dma((3,)), dma((3,)), dma((3,)),
            dma((2, parts_of_frame())), dma((2, parts_of_frame())), dma((3,)),
        ],
        compiler_params=pltpu.CompilerParams(
            collective_id=0, has_side_effects=True, vmem_limit_bytes=58 * 2**20
        ),
        name="guided_block",
    )(
        latents.reshape(PIX, C),
        norm_gain.reshape(1, C),
        second_gain.reshape(1, C),
        mine,
        critic_w.reshape(C, C),
        jnp.broadcast_to(critic_head, (8, C)),
        same,
        targets.reshape(-1),
        feasible.reshape(-1),
    )
    return guided.reshape(latents.shape)


def parts_of_frame():
    return 4


def solution(mesh):
    in_specs = (
        P("batch", "fsdp", None, None),
        P(),
        P(),
        P(None, None, "fsdp"),
        P(None, None, "fsdp"),
        P("batch", None, None),
        P("batch", None),
        P("batch", None, None),
        P("batch", "fsdp"),
    )
    body = fused if dict(mesh.shape) == {"fsdp": 8, "batch": 4} else per_device
    out_specs = P("batch", "fsdp", None, None)
    return jax.shard_map(
        body, mesh=mesh, in_specs=in_specs, out_specs=out_specs, check_vma=False
    )
```
